512 devices in a mesh: ctx: 128 (over y, z, core), tp: 4 (over x).
Axes of the slice: x: 4, y: 8, z: 8, core: 2. Of those that a mesh axis runs over, the one named last changes fastest.
Arguments:
- queries: bfloat16 [32768, 3072], P('ctx', 'tp'), may hold values from -24 to 24
- keys: bfloat16 [32768, 1024], P('ctx', 'tp'), may hold values from -6 to 6
- values: bfloat16 [32768, 1024], P('ctx', 'tp'), may hold values from -6 to 6
- doc_lengths: int32 [16], replicated, may hold values from 1 to 8192, 32768 in all
Outputs:
- attended: bfloat16 [32768, 3072], P(('ctx', 'tp'))
- log_total: float32 [24, 32768], P('tp', 'ctx')
The draws below stay inside these ranges and needn't reach their ends.
Inputs may be any that keep to these rules, and one draw needn't show every extreme that they name: `doc_lengths`: the lengths sum to 32768; one of them is exactly 8192.
All inputs are finite; a program needn't handle non-finite values.
Results may differ from the reference program's by a relative error of at most 0.0054.
Values may be sent and summed in bfloat16 or wider, within the bound.
A program may use at most 64 MiB of HBM per device.

```python
import math
import jax
import jax.numpy as jnp
import numpy as np
from jax import lax

HEADS = 24
KV_HEADS = 8
HEAD_DIM = 128
DOCS = 16
TOKENS = 32768
MOST_DOC = 8192


def draw_keys(key, part):
    own_key = jax.random.fold_in(key, 3)
    natural_keys = jnp.clip(jax.random.normal(own_key, (TOKENS, KV_HEADS * HEAD_DIM), jnp.float32), -6.0, 6.0)
    return natural_keys.astype(jnp.bfloat16)


def draw_queries(key, part):
    own_key = jax.random.fold_in(key, 5)
    natural_queries = jnp.clip(jax.random.normal(own_key, (TOKENS, HEADS * HEAD_DIM), jnp.float32), -6.0, 6.0)
    return natural_queries.astype(jnp.bfloat16)


def block_scale(stream_key, extent, split, smallest, largest):
    loudness = 1.0
    for dim, parts in split:
        heights = jax.random.uniform(jax.random.fold_in(jax.random.fold_in(stream_key, 6), dim), (parts,), jnp.float32, smallest / len(split), largest / len(split))
        loudness = loudness * jnp.repeat(jnp.exp(heights), extent[dim] // parts).reshape((-1,) + (1,) * (len(extent) - 1 - dim))
    return loudness


def profile(number_of, total, bound, slope):
    portions = [(1 << 20) // math.isqrt(standing ** slope) + 1 for standing in range(2, number_of + 1)]
    spare, counts = total - bound - (number_of - 1), [1] * (number_of - 1)
    while spare > 0:
        candidates = [i for i in range(number_of - 1) if counts[i] < bound]
        pool, remaining = sum([portions[i] for i in candidates]), spare
        for i in candidates:
            more = min(bound - counts[i], max(1, remaining * portions[i] // pool), spare)
            counts[i] = counts[i] + more
            spare = spare - more
    return np.array([bound] + counts)


def uneven_parts(key, amount, total, most, lean):
    if amount == 2:
        one = jax.random.randint(key, (), max(1, total - most), min(most, total - 1) + 1)
        return jnp.stack([one, total - one])
    sizes = jnp.asarray(profile(amount, total, most, lean), jnp.int32)
    pairs = (amount - 1) // 2
    source_of, sink = sizes[1:1 + 2 * pairs:2], sizes[2:2 + 2 * pairs:2]
    slack = jnp.minimum(source_of - 1, most - sink)
    shifted = jax.random.randint(jax.random.fold_in(key, 1), (pairs,), 0, 1 << 20) % (slack + 1)
    sizes = sizes.at[1:1 + 2 * pairs:2].set(source_of - shifted).at[2:2 + 2 * pairs:2].set(sink + shifted)
    return sizes[jax.random.permutation(jax.random.fold_in(key, 2), amount)]


def noise(stream_key, dims, scale, most, split=(), kind=jnp.bfloat16):
    result = scale * jax.random.normal(stream_key, dims, jnp.float32)
    if split:
        result = result * block_scale(stream_key, dims, split, -0.22, 0.18)
    return jnp.clip(result, -most, most).astype(kind)


def setup_inputs(seed: int = 0) -> dict:
    seeds = jax.random.split(jax.random.key(seed), 5)
    return {
        "queries": draw_queries(jax.random.fold_in(seeds[4], 71), 0),
        "keys": draw_keys(jax.random.fold_in(seeds[4], 71), 0),
        "values": noise(seeds[2], (TOKENS, KV_HEADS * HEAD_DIM), 1.0, 6.0, ((0, 128), (1, 4))),
        "doc_lengths": uneven_parts(seeds[3], DOCS, TOKENS, MOST_DOC, 2).astype(jnp.int32),
    }


NEG_FILL = -1e+30

def reference(queries, keys, values, doc_lengths):
    token_count = queries.shape[0]
    group_size = HEADS // KV_HEADS
    natural = jnp.arange(token_count, dtype=jnp.int32)
    query_nat = queries.astype(jnp.float32).reshape(token_count, KV_HEADS, group_size, HEAD_DIM)
    key_nat = keys.astype(jnp.float32).reshape(token_count, KV_HEADS, HEAD_DIM)
    value_nat = values.astype(jnp.float32).reshape(token_count, KV_HEADS, HEAD_DIM)
    doc_ends = jnp.cumsum(doc_lengths)
    doc_index = lax.optimization_barrier(jnp.sum((natural[:, None] >= doc_ends[None, :]).astype(jnp.int32), axis=1))
    query_rows = math.gcd(256, token_count)
    window = min(token_count, MOST_DOC + query_rows)
    score_scale = 1.0 / math.sqrt(HEAD_DIM)

    def one_block(block_number):
        first_row = block_number * query_rows
        key_first = jnp.clip(first_row + query_rows - window, 0, token_count - window).astype(jnp.int32)
        query_block = lax.dynamic_slice_in_dim(query_nat, first_row, query_rows, 0)
        key_block = lax.dynamic_slice_in_dim(key_nat, key_first, window, 0)
        value_block = lax.dynamic_slice_in_dim(value_nat, key_first, window, 0)
        query_pos = first_row + jnp.arange(query_rows, dtype=jnp.int32)
        key_pos = key_first + jnp.arange(window, dtype=jnp.int32)
        query_doc = lax.dynamic_slice_in_dim(doc_index, first_row, query_rows, 0)
        key_doc = lax.dynamic_slice_in_dim(doc_index, key_first, window, 0)
        allowed = (query_doc[:, None] == key_doc[None, :]) & (key_pos[None, :] <= query_pos[:, None])
        scores = jnp.einsum('qhgd,khd->hgqk', query_block, key_block, precision=lax.Precision.HIGHEST) * score_scale
        mask_full = allowed[None, None]
        peak = lax.optimization_barrier(jnp.max(jnp.where(mask_full, scores, NEG_FILL), axis=-1))
        weights = jnp.where(mask_full, jnp.exp(scores - peak[..., None]), 0.0)
        totals = lax.optimization_barrier(jnp.sum(weights, axis=-1))
        rounded = lax.optimization_barrier(weights.astype(jnp.bfloat16)).astype(jnp.float32)
        summed = jnp.einsum('hgqk,khd->qhgd', rounded, value_block, precision=lax.Precision.HIGHEST)
        output_block = (summed / jnp.transpose(totals, (2, 0, 1))[..., None]).astype(jnp.bfloat16)
        log_block = (peak + jnp.log(totals)).reshape(HEADS, query_rows)
        return (output_block.reshape(query_rows, HEADS * HEAD_DIM), log_block)
    outputs, logs = lax.map(one_block, jnp.arange(token_count // query_rows, dtype=jnp.int32))
    attended = outputs.reshape(token_count, HEADS * HEAD_DIM)
    log_total = jnp.transpose(logs, (1, 0, 2)).reshape(HEADS, token_count)
    return (attended, log_total)
```

```python
import math

import jax
import jax.numpy as jnp
from jax import lax
from jax.experimental import pallas as pl
from jax.experimental.pallas import tpu as pltpu
from jax.sharding import PartitionSpec as P

MESH = pl.DeviceIdType.MESH
HEAD_DIM = 128
GROUP = 3
ROWS = 256
CHUNK = 256
DOCS = 16
NEG = -1e30
SCALE = 1.0 / math.sqrt(HEAD_DIM)
TO_EXP2 = SCALE / math.log(2.0)

ARRIVALS = (
    (
        (63, 0, 2, 4, 6, 8, 10, 12),
        (63, 1, 3, 5, 7, 9, 11, 13),
        (30, 16, 0, 2, 4, 6, 8, 10),
        (31, 17, 1, 3, 5, 7, 9, 11),
        (28, 30, 16, 0, 2, 4, 6, 8),
        (29, 31, 18, 1, 3, 5, 7, 9),
        (26, 28, 30, 21, 0, 2, 4, 6),
        (27, 29, 31, 18, 1, 3, 5, 7),
        (24, 26, 19, 30, 40, 21, 2, 4),
        (25, 27, 17, 31, 16, 43, 3, 5),
        (46, 63, 46, 19, 18, 44, 21, 2),
        (47, 43, 63, 63, 63, 63, 63, 3),
    ),
    (
        (63, 63, 63, 63, 63, 63, 63, 0),
        (63, 63, 63, 63, 63, 63, 63, 1),
        (18, 20, 22, 24, 26, 28, 30, 16),
        (19, 21, 23, 25, 27, 29, 31, 17),
        (20, 22, 24, 26, 28, 30, 0, 18),
        (21, 23, 25, 27, 29, 31, 1, 19),
        (22, 24, 26, 28, 30, 0, 17, 20),
        (23, 25, 27, 29, 31, 1, 18, 21),
        (38, 40, 28, 43, 45, 17, 20, 22),
        (39, 41, 29, 44, 46, 18, 19, 23),
        (40, 42, 63, 45, 17, 20, 16, 63),
        (41, 63, 44, 63, 63, 19, 63, 63),
    ),
    (
        (16, 18, 20, 22, 24, 26, 28, 30),
        (17, 19, 21, 23, 25, 27, 29, 31),
        (32, 34, 36, 38, 22, 24, 26, 28),
        (33, 35, 37, 20, 23, 25, 27, 29),
        (34, 36, 38, 40, 42, 22, 24, 26),
        (35, 37, 39, 41, 21, 23, 25, 27),
        (36, 38, 40, 39, 43, 45, 22, 24),
        (37, 39, 41, 16, 44, 46, 23, 25),
        (42, 46, 42, 42, 41, 42, 47, 46),
        (43, 47, 43, 17, 19, 16, 45, 47),
        (44, 45, 47, 46, 20, 47, 44, 63),
        (45, 44, 45, 47, 47, 63, 46, 63),
    ),
)
NONE = 63
SLOTS = len(ARRIVALS[0])
PER_WORD = 5
BITS = 6


def departures(link):
    table = ARRIVALS[link]
    if link == 0:
        return [[row[(z + 1) % 8] for z in range(8)] for row in table]
    if link == 1:
        return [[row[(z - 1) % 8] for z in range(8)] for row in table]
    return [[v if v == NONE else v - 16 for v in row] for row in table]


def packed_words(table, z):
    words = []
    for first in range(0, SLOTS, PER_WORD):
        word = jnp.int32(0)
        for k in range(8):
            const = 0
            for i, row in enumerate(table[first : first + PER_WORD]):
                const += row[k] << (BITS * i)
            word = jnp.where(z == k, jnp.int32(const), word)
        words.append(word)
    return words


def look_up(words, slot):
    word = words[-1]
    for i in range(len(words) - 2, -1, -1):
        word = jnp.where(slot < (i + 1) * PER_WORD, words[i], word)
    return lax.shift_right_logical(word, BITS * lax.rem(slot, PER_WORD)) & (2**BITS - 1)


def kernel(
    q_ref, k_ref, v_ref, len_ref, out_ref, log_ref,
    buf, q_other, q_t, acc, peak, total, starts, staged, log_out, log_in,
    send_sem, recv_sem, trade_send, trade_recv, out_send, out_recv, log_sem,
):
    ctx, x = lax.axis_index("ctx"), lax.axis_index("tp")
    core, z, y = lax.rem(ctx, 2), lax.rem(ctx // 2, 8), ctx // 16

    def device(dy=0, dz=0, dcore=0, dx=0):
        yy, zz = lax.rem(y + dy + 8, 8), lax.rem(z + dz + 8, 8)
        return ((yy * 8 + zz) * 2 + lax.rem(core + dcore, 2), lax.rem(x + dx, 4))

    link_to = (device(dz=1), device(dz=-1), device(dy=1))

    barrier = pltpu.get_barrier_semaphore()
    senders = [device(dz=-1), device(dz=1), device(dy=-1)]
    senders += [device(dcore=h, dx=dx) for h in range(2) for dx in range(4) if h + dx]
    for d in senders:
        pl.semaphore_signal(barrier, inc=1, device_id=d, device_id_type=MESH)

    own = z * 2
    mine = pl.ds(pl.multiple_of(core * HEAD_DIM, HEAD_DIM), HEAD_DIM)
    theirs = pl.ds(pl.multiple_of((1 - core) * HEAD_DIM, HEAD_DIM), HEAD_DIM)
    width = GROUP * HEAD_DIM
    theirs_q = pl.ds(pl.multiple_of((1 - core) * width, HEAD_DIM), width)
    buf[own, :CHUNK, :] = k_ref[:, mine]
    buf[own, CHUNK:, :] = v_ref[:, mine]

    rx = [packed_words(ARRIVALS[link], z) for link in range(3)]
    tx = [packed_words(departures(link), z) for link in range(3)]

    pl.semaphore_wait(barrier, len(senders))

    other = device(dcore=1)

    def trade(i, src, dst):
        return pltpu.make_async_remote_copy(
            src_ref=src, dst_ref=dst, send_sem=trade_send.at[i], recv_sem=trade_recv.at[i],
            device_id=other, device_id_type=MESH,
        )

    trades = [
        trade(0, k_ref.at[:, theirs], buf.at[own + 1, pl.ds(0, CHUNK)]),
        trade(1, v_ref.at[:, theirs], buf.at[own + 1, pl.ds(CHUNK, CHUNK)]),
        trade(2, q_ref.at[:, theirs_q], q_other),
    ]

    def move(link, slot, chunk):
        landing = chunk + 16 if link == 2 else chunk
        return pltpu.make_async_remote_copy(
            src_ref=buf.at[chunk], dst_ref=buf.at[landing],
            send_sem=send_sem.at[link, slot], recv_sem=recv_sem.at[link, slot],
            device_id=link_to[link], device_id_type=MESH,
        )

    def send(slot):
        for link in range(3):
            chunk = look_up(tx[link], slot)

            @pl.when(chunk != NONE)
            def _(link=link, chunk=chunk):
                move(link, slot, chunk).start()

    for t in trades:
        t.start()
    send(jnp.int32(0))

    for half in range(2):
        base = (ctx - core) * ROWS + lax.rem(core + half, 2) * ROWS
        q_pos = base + lax.broadcasted_iota(jnp.int32, (1, ROWS), 1)
        start = jnp.zeros((1, ROWS), jnp.int32)
        end = jnp.int32(0)
        for i in range(DOCS):
            end = end + len_ref[i]
            start = jnp.where(q_pos >= end, end, start)
        starts[half : half + 1, :] = start
        starts[2 + half : 3 + half, :] = q_pos

    for g in range(GROUP):
        cols = pl.ds(pl.multiple_of(core * width + g * HEAD_DIM, HEAD_DIM), HEAD_DIM)
        q_t[:, 2 * g * ROWS : (2 * g + 1) * ROWS] = q_ref[:, cols].T

    trades[0].wait_recv()
    trades[1].wait_recv()
    send(jnp.int32(1))
    trades[2].wait_recv()
    for g in range(GROUP):
        q_t[:, (2 * g + 1) * ROWS : (2 * g + 2) * ROWS] = q_other[
            :, g * HEAD_DIM : (g + 1) * HEAD_DIM
        ].T

    def attend(chunks, first):
        keys, values, positions = [], [], []
        for chunk, base in chunks:
            keys.append(buf[chunk, :CHUNK, :])
            values.append(buf[chunk, CHUNK:, :].T)
            positions.append(base + lax.broadcasted_iota(jnp.int32, (CHUNK, ROWS), 0))
        for b in range(2 * GROUP):
            half = b % 2
            cols = slice(b * ROWS, (b + 1) * ROWS)
            start = starts[half : half + 1, :]
            scores = []
            for k, pos in zip(keys, positions):
                s = jnp.dot(k, q_t[:, cols], preferred_element_type=jnp.float32)
                allowed = pos >= start
                if first:
                    allowed = allowed & (pos <= starts[2 + half : 3 + half, :])
                scores.append(jnp.where(allowed, s, NEG))
            top = scores[0]
            for s in scores[1:]:
                top = jnp.maximum(top, s)
            top = jnp.max(top, axis=0, keepdims=True)
            if not first:
                before = peak[b : b + 1, :]
                top = jnp.maximum(top, before)
                factor = jnp.exp2((before - top) * TO_EXP2)
            summed, update = None, None
            for s, v in zip(scores, values):
                w = jnp.exp2((s - top) * TO_EXP2)
                part = jnp.dot(v, w.astype(jnp.bfloat16), preferred_element_type=jnp.float32)
                summed = w if summed is None else summed + w
                update = part if update is None else update + part
            summed = jnp.sum(summed, axis=0, keepdims=True)
            if not first:
                summed = summed + total[b : b + 1, :] * factor
                update = update + acc[:, cols] * factor
            peak[b : b + 1, :] = top
            total[b : b + 1, :] = summed
            acc[:, cols] = update

    def base_of(chunk):
        back, s, part = chunk // 16, lax.rem(chunk // 2, 8), lax.rem(chunk, 2)
        base = (((y - back) * 8 + s) * 2 + lax.rem(part + core, 2)) * ROWS
        return jnp.where(chunk == NONE, -ROWS, base)

    attend([(own, base_of(own)), (own + 1, base_of(own + 1))], True)

    def step(slot, carry):
        chunks = []
        for link in range(3):
            chunk = look_up(rx[link], slot)
            safe = jnp.where(chunk == NONE, own, chunk)

            @pl.when(chunk != NONE)
            def _(link=link, safe=safe):
                pltpu.make_async_remote_copy(
                    src_ref=buf.at[safe], dst_ref=buf.at[safe],
                    send_sem=send_sem.at[link, slot], recv_sem=recv_sem.at[link, slot],
                    device_id=link_to[link], device_id_type=MESH,
                ).wait_recv()

            chunks.append((safe, base_of(chunk)))

        @pl.when(slot + 2 < SLOTS)
        def _():
            send(slot + 2)

        attend(chunks, False)
        return carry

    lax.fori_loop(0, SLOTS, step, 0)

    for b in range(2 * GROUP):
        g, half = b // 2, b % 2
        sums = total[b : b + 1, :]
        o = (acc[:, b * ROWS : (b + 1) * ROWS] / sums).T
        staged[half * ROWS : (half + 1) * ROWS, g * HEAD_DIM : (g + 1) * HEAD_DIM] = o.astype(
            jnp.bfloat16
        )
        log_out[half, g : g + 1, :] = peak[b : b + 1, :] * SCALE + jnp.log(sums)

    share = ROWS // 4
    spot = pl.ds(pl.multiple_of((2 * x + core) * width, HEAD_DIM), width)
    sends = []
    for half in range(2):
        for dx in range(4):
            if half + dx == 0:
                continue
            to = lax.rem(x + dx, 4)
            copy = pltpu.make_async_remote_copy(
                src_ref=staged.at[pl.ds(pl.multiple_of(half * ROWS + to * share, share), share)],
                dst_ref=out_ref.at[:, spot],
                send_sem=out_send.at[half, dx], recv_sem=out_recv.at[half, dx],
                device_id=device(dcore=half, dx=dx), device_id_type=MESH,
            )
            copy.start()
            sends.append(copy)
    log_copy = pltpu.make_async_remote_copy(
        src_ref=log_out.at[1], dst_ref=log_in, send_sem=log_sem.at[0], recv_sem=log_sem.at[1],
        device_id=other, device_id_type=MESH,
    )
    log_copy.start()
    out_ref[:, spot] = staged[pl.ds(pl.multiple_of(x * share, share), share), :]
    log_copy.wait()
    near, far = log_out[0, :GROUP, :], log_in[:GROUP, :]
    log_ref[:GROUP, :] = jnp.where(core == 0, near, far)
    log_ref[GROUP:, :] = jnp.where(core == 0, far, near)

    for t in trades:
        t.wait_send()

    def drain(slot, carry):
        for link in range(3):
            chunk = look_up(tx[link], slot)

            @pl.when(chunk != NONE)
            def _(link=link, chunk=chunk):
                move(link, slot, chunk).wait_send()

        return carry

    lax.fori_loop(0, SLOTS, drain, 0)
    for copy in sends:
        copy.wait()


def on_device(queries, keys, values, doc_lengths):
    columns = 4 * queries.shape[1]
    dma = pltpu.SemaphoreType.DMA
    vmem = pl.BlockSpec(memory_space=pltpu.VMEM)
    return pl.pallas_call(
        kernel,
        out_shape=(
            jax.ShapeDtypeStruct((ROWS // 4, columns), jnp.bfloat16),
            jax.ShapeDtypeStruct((2 * GROUP, ROWS), jnp.float32),
        ),
        in_specs=[vmem, vmem, vmem, pl.BlockSpec(memory_space=pltpu.SMEM)],
        out_specs=(vmem, vmem),
        scratch_shapes=[
            pltpu.VMEM((48, 2 * CHUNK, HEAD_DIM), jnp.bfloat16),
            pltpu.VMEM((ROWS, GROUP * HEAD_DIM), jnp.bfloat16),
            pltpu.VMEM((HEAD_DIM, 2 * GROUP * ROWS), jnp.bfloat16),
            pltpu.VMEM((HEAD_DIM, 2 * GROUP * ROWS), jnp.float32),
            pltpu.VMEM((8, ROWS), jnp.float32),
            pltpu.VMEM((8, ROWS), jnp.float32),
            pltpu.VMEM((8, ROWS), jnp.int32),
            pltpu.VMEM((2 * ROWS, GROUP * HEAD_DIM), jnp.bfloat16),
            pltpu.VMEM((2, 8, ROWS), jnp.float32),
            pltpu.VMEM((8, ROWS), jnp.float32),
            dma((3, SLOTS)),
            dma((3, SLOTS)),
            dma((3,)),
            dma((3,)),
            dma((2, 4)),
            dma((2, 4)),
            dma((2,)),
        ],
        compiler_params=pltpu.CompilerParams(
            collective_id=0, has_side_effects=True, vmem_limit_bytes=48 * 2**20
        ),
        cost_estimate=pl.CostEstimate(
            flops=8 * 10**9, bytes_accessed=2 * 10**6, transcendentals=14 * 10**6
        ),
    )(queries, keys, values, doc_lengths)


def solution(mesh):
    in_specs = (P("ctx", "tp"), P("ctx", "tp"), P("ctx", "tp"), P())
    out_specs = (P(("ctx", "tp"), None), P("tp", "ctx"))
    return jax.shard_map(
        on_device, mesh=mesh, in_specs=in_specs, out_specs=out_specs, check_vma=False
    )
```

```python
import math

import jax
import jax.numpy as jnp
from jax import lax
from jax.experimental import pallas as pl
from jax.experimental.pallas import tpu as pltpu
from jax.sharding import PartitionSpec as P

MESH = pl.DeviceIdType.MESH
HEAD_DIM = 128
GROUP = 3
ROWS = 256
CHUNK = 256
DOCS = 16
NEG = -1e30
APART = 2.0**20
SCALE = 1.0 / math.sqrt(HEAD_DIM)
TO_EXP2 = SCALE / math.log(2.0)

ARRIVALS = (
    (
        (63, 0, 2, 4, 6, 8, 10, 12),
        (63, 1, 3, 5, 7, 9, 11, 13),
        (30, 16, 0, 2, 4, 6, 8, 10),
        (31, 17, 1, 3, 5, 7, 9, 11),
        (28, 30, 16, 0, 2, 4, 6, 8),
        (29, 31, 18, 1, 3, 5, 7, 9),
        (26, 28, 30, 21, 0, 2, 4, 6),
        (27, 29, 31, 18, 1, 3, 5, 7),
        (24, 26, 19, 30, 40, 21, 2, 4),
        (25, 27, 17, 31, 16, 43, 3, 5),
        (46, 63, 46, 19, 18, 44, 21, 2),
        (47, 43, 63, 63, 63, 63, 63, 3),
    ),
    (
        (63, 63, 63, 63, 63, 63, 63, 0),
        (63, 63, 63, 63, 63, 63, 63, 1),
        (18, 20, 22, 24, 26, 28, 30, 16),
        (19, 21, 23, 25, 27, 29, 31, 17),
        (20, 22, 24, 26, 28, 30, 0, 18),
        (21, 23, 25, 27, 29, 31, 1, 19),
        (22, 24, 26, 28, 30, 0, 17, 20),
        (23, 25, 27, 29, 31, 1, 18, 21),
        (38, 40, 28, 43, 45, 17, 20, 22),
        (39, 41, 29, 44, 46, 18, 19, 23),
        (40, 42, 63, 45, 17, 20, 16, 63),
        (41, 63, 44, 63, 63, 19, 63, 63),
    ),
    (
        (16, 18, 20, 22, 24, 26, 28, 30),
        (17, 19, 21, 23, 25, 27, 29, 31),
        (32, 34, 36, 38, 22, 24, 26, 28),
        (33, 35, 37, 20, 23, 25, 27, 29),
        (34, 36, 38, 40, 42, 22, 24, 26),
        (35, 37, 39, 41, 21, 23, 25, 27),
        (36, 38, 40, 39, 43, 45, 22, 24),
        (37, 39, 41, 16, 44, 46, 23, 25),
        (42, 46, 42, 42, 41, 42, 47, 46),
        (43, 47, 43, 17, 19, 16, 45, 47),
        (44, 45, 47, 46, 20, 47, 44, 63),
        (45, 44, 45, 47, 47, 63, 46, 63),
    ),
)
NONE = 63
SLOTS = len(ARRIVALS[0])
PER_WORD = 5
BITS = 6


def departures(link):
    table = ARRIVALS[link]
    if link == 0:
        return [[row[(z + 1) % 8] for z in range(8)] for row in table]
    if link == 1:
        return [[row[(z - 1) % 8] for z in range(8)] for row in table]
    return [[v if v == NONE else v - 16 for v in row] for row in table]


def packed_words(table, z):
    words = []
    for first in range(0, SLOTS, PER_WORD):
        word = jnp.int32(0)
        for k in range(8):
            const = 0
            for i, row in enumerate(table[first : first + PER_WORD]):
                const += row[k] << (BITS * i)
            word = jnp.where(z == k, jnp.int32(const), word)
        words.append(word)
    return words


def look_up(words, slot):
    word = words[-1]
    for i in range(len(words) - 2, -1, -1):
        word = jnp.where(slot < (i + 1) * PER_WORD, words[i], word)
    return lax.shift_right_logical(word, BITS * lax.rem(slot, PER_WORD)) & (2**BITS - 1)


def kernel(
    q_ref, k_ref, v_ref, len_ref, out_ref, log_ref,
    buf, q_near, q_far, q_all, acc, peak, bounds, lengths, staged, log_out, log_in,
    send_sem, recv_sem, local_sem, trade_send, trade_recv, out_send, out_recv, log_sem,
):
    ctx, x = lax.axis_index("ctx"), lax.axis_index("tp")
    core, z, y = lax.rem(ctx, 2), lax.rem(ctx // 2, 8), ctx // 16

    def device(dy=0, dz=0, dcore=0, dx=0):
        yy, zz = lax.rem(y + dy + 8, 8), lax.rem(z + dz + 8, 8)
        return ((yy * 8 + zz) * 2 + lax.rem(core + dcore, 2), lax.rem(x + dx, 4))

    link_to = (device(dz=1), device(dz=-1), device(dy=1))

    barrier = pltpu.get_barrier_semaphore()
    senders = [device(dz=-1), device(dz=1), device(dy=-1)]
    senders += [device(dcore=h, dx=dx) for h in range(2) for dx in range(4) if h + dx]
    for d in senders:
        pl.semaphore_signal(barrier, inc=1, device_id=d, device_id_type=MESH)

    own = z * 2
    width = GROUP * HEAD_DIM
    mine = pl.ds(pl.multiple_of(core * HEAD_DIM, HEAD_DIM), HEAD_DIM)
    theirs = pl.ds(pl.multiple_of((1 - core) * HEAD_DIM, HEAD_DIM), HEAD_DIM)
    mine_q = pl.ds(pl.multiple_of(core * width, HEAD_DIM), width)
    theirs_q = pl.ds(pl.multiple_of((1 - core) * width, HEAD_DIM), width)
    local = [
        pltpu.make_async_copy(src, dst, local_sem.at[i])
        for i, (src, dst) in enumerate(
            (
                (k_ref.at[:, mine], buf.at[own, pl.ds(0, CHUNK)]),
                (v_ref.at[:, mine], buf.at[own, pl.ds(CHUNK, CHUNK)]),
                (q_ref.at[:, mine_q], q_near),
                (len_ref, lengths),
            )
        )
    ]
    for copy in local:
        copy.start()

    rx = [packed_words(ARRIVALS[link], z) for link in range(3)]
    tx = [packed_words(departures(link), z) for link in range(3)]

    other = device(dcore=1)

    def trade(i, src, dst):
        return pltpu.make_async_remote_copy(
            src_ref=src, dst_ref=dst, send_sem=trade_send.at[i], recv_sem=trade_recv.at[i],
            device_id=other, device_id_type=MESH,
        )

    trades = [
        trade(0, k_ref.at[:, theirs], buf.at[own + 1, pl.ds(0, CHUNK)]),
        trade(1, v_ref.at[:, theirs], buf.at[own + 1, pl.ds(CHUNK, CHUNK)]),
        trade(2, q_ref.at[:, theirs_q], q_far),
    ]

    def move(link, slot, chunk):
        landing = chunk + 16 if link == 2 else chunk
        return pltpu.make_async_remote_copy(
            src_ref=buf.at[chunk], dst_ref=buf.at[landing],
            send_sem=send_sem.at[link, slot], recv_sem=recv_sem.at[link, slot],
            device_id=link_to[link], device_id_type=MESH,
        )

    def leaving(link, slot):
        chunk = look_up(tx[link], slot)
        there = (chunk != NONE) & (chunk // 16 <= y)
        return chunk, (there & (y < 7)) if link == 2 else there

    def send(slot):
        for link in range(3):
            chunk, there = leaving(link, slot)

            @pl.when(there)
            def _(link=link, chunk=chunk):
                move(link, slot, chunk).start()

    pl.semaphore_wait(barrier, len(senders))
    trades[0].start()
    trades[1].start()
    local[0].wait()
    local[1].wait()
    send(jnp.int32(0))
    trades[2].start()

    local[3].wait()
    lane = lax.broadcasted_iota(jnp.int32, (1, HEAD_DIM), 1)
    starts = jnp.zeros((1, HEAD_DIM), jnp.int32)
    ends = jnp.zeros((1, HEAD_DIM), jnp.int32)
    end = jnp.int32(0)
    for i in range(DOCS):
        starts = jnp.where(lane == i, end, starts)
        end = end + lengths[i]
        ends = jnp.where(lane == i, end, ends)
    bounds[0:1, :] = starts
    bounds[1:2, :] = ends

    def in_document(base):
        pos = base + lax.broadcasted_iota(jnp.int32, (CHUNK, HEAD_DIM), 0)
        return (pos >= bounds[0:1, :]) & (pos < bounds[1:2, :])

    q_base = [(ctx - core + lax.rem(core + half, 2)) * ROWS for half in range(2)]
    for half in range(2):
        one_hot = jnp.where(in_document(q_base[half]), 1.0, 0.0).astype(jnp.bfloat16)
        for g in range(GROUP):
            b = 2 * g + half
            q_all[b * ROWS : (b + 1) * ROWS, HEAD_DIM:] = one_hot
    local[2].wait()
    trades[0].wait_recv()
    trades[1].wait_recv()
    send(jnp.int32(1))
    trades[2].wait_recv()
    for half, q_half in enumerate((q_near, q_far)):
        for g in range(GROUP):
            b = 2 * g + half
            q_all[b * ROWS : (b + 1) * ROWS, :HEAD_DIM] = q_half[
                :, g * HEAD_DIM : (g + 1) * HEAD_DIM
            ]

    halves = (slice(0, HEAD_DIM), slice(HEAD_DIM, 2 * HEAD_DIM))

    def load(chunks):
        keys, values = [], []
        for chunk, base in chunks:
            apart = jnp.where(in_document(base), 0.0, -APART).astype(jnp.bfloat16)
            keys.append(jnp.concatenate([buf[chunk, :CHUNK, :], apart], axis=1))
            ones = jnp.ones((CHUNK, HEAD_DIM), jnp.bfloat16)
            values.append(jnp.concatenate([buf[chunk, CHUNK:, :], ones], axis=1))
        return keys, jnp.concatenate(values, axis=0)

    def attend(b, keys, values, bases=None):
        rows = slice(b * ROWS, (b + 1) * ROWS)
        q = q_all[rows, :]
        scores = []
        for i, k in enumerate(keys):
            s = lax.dot_general(
                q, k, (((1,), (1,)), ((), ())), preferred_element_type=jnp.float32
            )
            if bases is not None:
                q_pos = q_base[b % 2] + lax.broadcasted_iota(jnp.int32, (ROWS, CHUNK), 0)
                k_pos = bases[i] + lax.broadcasted_iota(jnp.int32, (ROWS, CHUNK), 1)
                s = jnp.where(k_pos <= q_pos, s, NEG)
            scores += [s[:, h] for h in halves]
        top = scores[0]
        for s in scores[1:]:
            top = jnp.maximum(top, s)
        top = jnp.max(top, axis=1, keepdims=True)
        if bases is None:
            before = peak[rows, :]
            top = jnp.maximum(before, top)
            factor = jnp.exp2((before - top) * TO_EXP2)
        else:
            top = jnp.broadcast_to(top, (ROWS, HEAD_DIM))
        weights = [jnp.exp2((s - top) * TO_EXP2).astype(jnp.bfloat16) for s in scores]
        update = jnp.dot(
            jnp.concatenate(weights, axis=1), values, preferred_element_type=jnp.float32
        )
        peak[rows, :] = top
        for h in halves:
            acc[rows, h] = update[:, h] if bases is not None else acc[rows, h] * factor + update[:, h]

    def base_of(chunk, there):
        back, s, part = chunk // 16, lax.rem(chunk // 2, 8), lax.rem(chunk, 2)
        base = (((y - back) * 8 + s) * 2 + lax.rem(part + core, 2)) * ROWS
        return jnp.where(there, base, -ROWS)

    bases = q_base
    keys, values = load([(own, bases[0]), (own + 1, bases[1])])
    for b in range(2 * GROUP):
        attend(b, keys, values, bases)

    def arrived(slot):
        chunks = []
        for link in range(3):
            chunk = look_up(rx[link], slot)
            there = (chunk != NONE) & (chunk // 16 <= y)
            safe = jnp.where(there, chunk, own)

            @pl.when(there)
            def _(link=link, safe=safe):
                pltpu.make_async_remote_copy(
                    src_ref=buf.at[safe], dst_ref=buf.at[safe],
                    send_sem=send_sem.at[link, slot], recv_sem=recv_sem.at[link, slot],
                    device_id=link_to[link], device_id_type=MESH,
                ).wait_recv()

            chunks.append((safe, base_of(chunk, there)))
        return chunks

    def step(slot, carry):
        chunks = arrived(slot)

        @pl.when(slot + 2 < SLOTS)
        def _():
            send(slot + 2)

        keys, values = load(chunks)
        for b in range(2 * GROUP):
            attend(b, keys, values)
        return carry

    lax.fori_loop(0, SLOTS - 1, step, 0)

    share = ROWS // 4
    sends = []
    keys, values = load(arrived(jnp.int32(SLOTS - 1)))
    for b in range(2 * GROUP):
        attend(b, keys, values)
        g, half = b // 2, b % 2
        rows = slice(b * ROWS, (b + 1) * ROWS)
        staged[rows, :] = (acc[rows, :HEAD_DIM] / acc[rows, HEAD_DIM:]).astype(jnp.bfloat16)
        spot = pl.ds(pl.multiple_of((2 * x + core) * width + g * HEAD_DIM, HEAD_DIM), HEAD_DIM)
        for dx in range(4):
            to = lax.rem(x + dx, 4)
            piece = pl.ds(pl.multiple_of(b * ROWS + to * share, share), share)
            if half + dx == 0:
                out_ref[:, spot] = staged[piece, :]
                continue
            copy = pltpu.make_async_remote_copy(
                src_ref=staged.at[piece], dst_ref=out_ref.at[:, spot],
                send_sem=out_send.at[b, dx], recv_sem=out_recv.at[b, dx],
                device_id=device(dcore=half, dx=dx), device_id_type=MESH,
            )
            copy.start()
            sends.append(copy)

    for b in (1, 3, 5, 0, 2, 4):
        rows = slice(b * ROWS, (b + 1) * ROWS)
        log = (peak[rows, :] * SCALE + jnp.log(acc[rows, HEAD_DIM:])).T
        log_out[b % 2, b // 2 : b // 2 + 1, :] = log[:1, :]
        if b == 5:
            log_copy = pltpu.make_async_remote_copy(
                src_ref=log_out.at[1], dst_ref=log_in,
                send_sem=log_sem.at[0], recv_sem=log_sem.at[1],
                device_id=other, device_id_type=MESH,
            )
            log_copy.start()

    for t in trades:
        t.wait_send()

    def drain(slot, carry):
        for link in range(3):
            chunk, there = leaving(link, slot)

            @pl.when(there)
            def _(link=link, chunk=chunk):
                move(link, slot, chunk).wait_send()

        return carry

    lax.fori_loop(0, SLOTS, drain, 0)
    log_copy.wait()
    near, far = log_out[0, :GROUP, :], log_in[:GROUP, :]
    log_ref[:GROUP, :] = jnp.where(core == 0, near, far)
    log_ref[GROUP:, :] = jnp.where(core == 0, far, near)
    for copy in sends:
        copy.wait()


def on_device(queries, keys, values, doc_lengths):
    columns = 4 * queries.shape[1]
    dma = pltpu.SemaphoreType.DMA
    bf16, f32 = jnp.bfloat16, jnp.float32
    vmem = pl.BlockSpec(memory_space=pltpu.VMEM)
    return pl.pallas_call(
        kernel,
        out_shape=(
            jax.ShapeDtypeStruct((ROWS // 4, columns), bf16),
            jax.ShapeDtypeStruct((2 * GROUP, ROWS), f32),
        ),
        in_specs=[pl.BlockSpec(memory_space=pltpu.HBM)] * 4,
        out_specs=(vmem, vmem),
        scratch_shapes=[
            pltpu.VMEM((48, 2 * CHUNK, HEAD_DIM), bf16),
            pltpu.VMEM((ROWS, GROUP * HEAD_DIM), bf16),
            pltpu.VMEM((ROWS, GROUP * HEAD_DIM), bf16),
            pltpu.VMEM((2 * GROUP * ROWS, 2 * HEAD_DIM), bf16),
            pltpu.VMEM((2 * GROUP * ROWS, 2 * HEAD_DIM), f32),
            pltpu.VMEM((2 * GROUP * ROWS, HEAD_DIM), f32),
            pltpu.VMEM((8, HEAD_DIM), jnp.int32),
            pltpu.SMEM((DOCS,), jnp.int32),
            pltpu.VMEM((2 * GROUP * ROWS, HEAD_DIM), bf16),
            pltpu.VMEM((2, 8, ROWS), f32),
            pltpu.VMEM((8, ROWS), f32),
            dma((3, SLOTS)),
            dma((3, SLOTS)),
            dma((4,)),
            dma((3,)),
            dma((3,)),
            dma((2 * GROUP, 4)),
            dma((2 * GROUP, 4)),
            dma((2,)),
        ],
        compiler_params=pltpu.CompilerParams(
            collective_id=0, has_side_effects=True, vmem_limit_bytes=int(63.9 * 2**20)
        ),
        cost_estimate=pl.CostEstimate(
            flops=8 * 10**9, bytes_accessed=2 * 10**6, transcendentals=14 * 10**6
        ),
    )(queries, keys, values, doc_lengths)


def solution(mesh):
    in_specs = (P("ctx", "tp"), P("ctx", "tp"), P("ctx", "tp"), P())
    out_specs = (P(("ctx", "tp"), None), P("tp", "ctx"))
    return jax.shard_map(
        on_device, mesh=mesh, in_specs=in_specs, out_specs=out_specs, check_vma=False
    )
```

```python
import math

import jax
import jax.numpy as jnp
from jax import lax
from jax.experimental import pallas as pl
from jax.experimental.pallas import tpu as pltpu
from jax.sharding import PartitionSpec as P

MESH = pl.DeviceIdType.MESH
HEAD_DIM = 128
GROUP = 3
ROWS = 256
CHUNK = 128
DOCS = 16
NEG = -1e30
APART = 2.0**20
SCALE = 1.0 / math.sqrt(HEAD_DIM)
TO_EXP2 = SCALE / math.log(2.0)

ARRIVALS = (
    (
        (127, 127, 127, 127, 127, 127, 127, 127),
        (127, 2, 127, 127, 127, 127, 127, 127),
        (127, 3, 5, 127, 127, 127, 127, 127),
        (127, 0, 6, 11, 127, 127, 127, 127),
        (127, 1, 4, 10, 14, 127, 127, 127),
        (127, 33, 7, 8, 15, 18, 20, 25),
        (127, 35, 2, 9, 13, 16, 23, 26),
        (127, 34, 0, 6, 12, 19, 22, 27),
        (127, 32, 1, 5, 10, 17, 21, 24),
        (61, 127, 3, 4, 8, 15, 18, 20),
        (60, 127, 37, 7, 9, 13, 16, 23),
        (62, 127, 39, 0, 11, 12, 19, 22),
        (63, 127, 34, 1, 6, 14, 17, 21),
        (57, 61, 35, 2, 4, 8, 15, 18),
        (58, 60, 33, 3, 7, 9, 13, 16),
        (59, 62, 36, 41, 5, 11, 12, 19),
        (56, 63, 127, 39, 1, 10, 14, 17),
        (52, 57, 61, 34, 0, 6, 8, 50),
        (55, 58, 60, 33, 3, 7, 9, 13),
        (54, 59, 62, 36, 2, 5, 11, 12),
        (53, 56, 63, 35, 39, 4, 10, 14),
        (50, 89, 93, 61, 34, 42, 6, 15),
        (48, 55, 58, 60, 37, 38, 7, 9),
        (51, 54, 57, 62, 36, 41, 5, 8),
        (94, 53, 127, 127, 32, 84, 4, 10),
        (95, 84, 89, 93, 82, 85, 91, 11),
        (127, 87, 90, 92, 35, 34, 38, 7),
        (127, 127, 127, 94, 127, 127, 42, 5),
        (127, 127, 127, 127, 127, 127, 127, 4),
        (127, 127, 127, 127, 127, 127, 127, 6),
    ),
    (
        (127, 127, 127, 127, 127, 127, 127, 127),
        (127, 127, 127, 127, 127, 127, 127, 127),
        (127, 127, 127, 127, 127, 127, 127, 127),
        (127, 127, 127, 127, 127, 127, 127, 127),
        (127, 127, 127, 127, 127, 127, 127, 127),
        (36, 127, 127, 127, 127, 127, 127, 3),
        (39, 40, 127, 127, 127, 127, 127, 2),
        (37, 43, 44, 127, 127, 127, 127, 0),
        (38, 41, 45, 49, 127, 127, 127, 1),
        (68, 42, 46, 51, 53, 56, 61, 35),
        (40, 127, 47, 50, 52, 59, 60, 34),
        (43, 44, 127, 48, 55, 57, 62, 36),
        (41, 45, 49, 127, 54, 58, 63, 32),
        (42, 74, 51, 53, 56, 61, 1, 38),
        (72, 47, 50, 52, 59, 60, 0, 33),
        (44, 46, 48, 55, 57, 62, 3, 43),
        (45, 49, 127, 54, 58, 63, 2, 40),
        (74, 51, 53, 56, 61, 1, 35, 37),
        (47, 50, 52, 59, 60, 0, 34, 92),
        (46, 48, 55, 57, 62, 3, 43, 44),
        (76, 81, 54, 58, 63, 2, 40, 42),
        (49, 83, 56, 84, 88, 35, 32, 39),
        (77, 82, 59, 87, 89, 45, 37, 41),
        (78, 80, 127, 40, 90, 43, 36, 46),
        (79, 52, 86, 63, 92, 95, 33, 47),
        (81, 85, 84, 127, 94, 40, 94, 127),
        (83, 127, 91, 127, 91, 93, 44, 127),
        (127, 127, 127, 127, 127, 37, 39, 127),
        (127, 127, 127, 127, 127, 127, 127, 127),
        (127, 127, 127, 127, 127, 127, 127, 127),
    ),
    (
        (33, 127, 127, 127, 127, 127, 127, 127),
        (35, 36, 127, 127, 127, 127, 127, 127),
        (32, 39, 40, 127, 127, 127, 127, 127),
        (34, 37, 43, 44, 127, 127, 127, 127),
        (65, 38, 41, 45, 49, 127, 127, 127),
        (67, 68, 42, 46, 51, 53, 56, 61),
        (64, 71, 72, 47, 50, 52, 59, 60),
        (66, 69, 75, 43, 48, 55, 57, 62),
        (127, 70, 73, 42, 46, 54, 58, 63),
        (127, 127, 74, 77, 47, 50, 52, 57),
        (71, 72, 38, 79, 45, 48, 55, 58),
        (69, 75, 76, 78, 44, 51, 54, 59),
        (70, 73, 77, 81, 42, 49, 53, 56),
        (93, 127, 78, 83, 85, 47, 50, 52),
        (92, 127, 79, 82, 84, 88, 48, 55),
        (75, 76, 32, 80, 87, 89, 51, 54),
        (73, 77, 81, 76, 86, 90, 49, 53),
        (89, 93, 83, 38, 40, 91, 47, 94),
        (90, 79, 82, 37, 38, 46, 45, 48),
        (91, 78, 80, 32, 41, 92, 93, 51),
        (88, 94, 127, 86, 33, 94, 95, 49),
        (84, 95, 85, 85, 93, 44, 46, 95),
        (87, 90, 92, 91, 43, 33, 89, 45),
        (86, 91, 94, 88, 83, 39, 90, 93),
        (85, 88, 95, 89, 80, 87, 88, 127),
        (82, 92, 87, 90, 81, 86, 92, 127),
        (80, 127, 88, 127, 95, 32, 41, 127),
        (127, 86, 127, 127, 127, 36, 127, 127),
        (127, 127, 127, 95, 127, 127, 127, 127),
        (127, 127, 127, 127, 127, 127, 127, 127),
    ),
)
STARTS = (0, 1, 2, 3, 4, 5, 5, 5)
NONE = 127
PARTS = 4
LEAD = 4
ROW = 8 * PARTS
PER_WORD = 4
BITS = 7
TOWARDS = (1, -1, 0)


def own_slots(link, leaving):
    table = ARRIVALS[link]
    rows = []
    for slot in range(len(table)):
        row = []
        for z in range(8):
            t, at = slot + STARTS[z], (z + TOWARDS[link]) % 8 if leaving else z
            v = table[t][at] if t < len(table) else NONE
            row.append(v - ROW if leaving and link == 2 and v != NONE else v)
        rows.append(row)
    while all(v == NONE for v in rows[-1]):
        rows.pop()
    return rows


COMING = [own_slots(link, False) for link in range(3)]
GOING = [own_slots(link, True) for link in range(3)]
SLOTS = max(len(table) for table in COMING)
SENDS = max(len(table) for table in GOING)
PAIRS = (SLOTS - 1) // 2


def first_slot(link, z):
    return min(t for t, row in enumerate(GOING[link]) if row[z] != NONE)


def packed_words(table, z):
    words = []
    table = table + [[NONE] * 8] * (-len(table) % PER_WORD)
    for first in range(0, len(table), PER_WORD):
        word = jnp.int32(0)
        for k in range(8):
            const = 0
            for i, row in enumerate(table[first : first + PER_WORD]):
                const += row[k] << (BITS * i)
            word = jnp.where(z == k, jnp.int32(const), word)
        words.append(word)
    return words


def look_up(words, slot):
    word = jnp.where(slot < len(words) * PER_WORD, words[-1], -1)
    for i in range(len(words) - 2, -1, -1):
        word = jnp.where(slot < (i + 1) * PER_WORD, words[i], word)
    return lax.shift_right_logical(word, BITS * lax.rem(slot, PER_WORD)) & (2**BITS - 1)


def kernel(
    q_ref, k_ref, v_ref, len_ref, out_ref, log_ref,
    buf, q_near, q_far, q_all, acc, peak, bounds, lengths, staged, log_out, log_in,
    send_sem, recv_sem, ready, local_sem, trade_send, trade_recv, out_send, out_recv, log_sem,
):
    ctx, x = lax.axis_index("ctx"), lax.axis_index("tp")
    core, z, y = lax.rem(ctx, 2), lax.rem(ctx // 2, 8), ctx // 16

    def device(dy=0, dz=0, dcore=0, dx=0):
        yy, zz = lax.rem(y + dy + 8, 8), lax.rem(z + dz + 8, 8)
        return ((yy * 8 + zz) * 2 + lax.rem(core + dcore, 2), lax.rem(x + dx, 4))

    link_to = (device(dz=1), device(dz=-1), device(dy=1))

    barrier = pltpu.get_barrier_semaphore()

    def signal(semaphore, to):
        pl.semaphore_signal(semaphore, inc=1, device_id=to, device_id_type=MESH)

    signal(barrier, device(dy=-1))
    for half in range(2):
        for dx in range(4):
            if half + dx:
                signal(barrier, device(dcore=half, dx=dx))

    @pl.when(z < 7)
    def _():
        signal(barrier, device(dz=1))

    @pl.when(z == 0)
    def _():
        signal(barrier, device(dz=-1))

    own = z * PARTS
    width = GROUP * HEAD_DIM
    mine = pl.ds(pl.multiple_of(core * HEAD_DIM, HEAD_DIM), HEAD_DIM)
    theirs = pl.ds(pl.multiple_of((1 - core) * HEAD_DIM, HEAD_DIM), HEAD_DIM)
    mine_q = pl.ds(pl.multiple_of(core * width, HEAD_DIM), width)
    theirs_q = pl.ds(pl.multiple_of((1 - core) * width, HEAD_DIM), width)
    local = []

    def bring(src, dst):
        local.append(pltpu.make_async_copy(src, dst, local_sem.at[len(local)]))

    def part(ref, i, columns):
        return ref.at[pl.ds(i * CHUNK, CHUNK), columns]

    for i in range(2):
        bring(part(k_ref, i, mine), buf.at[own + i, pl.ds(0, CHUNK)])
        bring(part(v_ref, i, mine), buf.at[own + i, pl.ds(CHUNK, CHUNK)])
    bring(q_ref.at[:, mine_q], q_near)
    bring(len_ref, lengths)
    for copy in local:
        copy.start()

    rx = [packed_words(COMING[link], z) for link in range(3)]
    tx = [packed_words(GOING[link], z) for link in range(3)]
    first_up = jnp.int32(-1)
    for k in range(7):
        first_up = jnp.where(z == k, first_slot(0, k), first_up)

    other = device(dcore=1)

    def trade(i, src, dst):
        return pltpu.make_async_remote_copy(
            src_ref=src, dst_ref=dst, send_sem=trade_send.at[i], recv_sem=trade_recv.at[i],
            device_id=other, device_id_type=MESH,
        )

    trades = []
    for i in range(2):
        trades.append(trade(2 * i, part(k_ref, i, theirs), buf.at[own + 2 + i, pl.ds(0, CHUNK)]))
        trades.append(
            trade(2 * i + 1, part(v_ref, i, theirs), buf.at[own + 2 + i, pl.ds(CHUNK, CHUNK)])
        )
    trades.append(trade(4, q_ref.at[:, theirs_q], q_far))

    def move(link, slot, chunk):
        landing = chunk + ROW if link == 2 else chunk
        return pltpu.make_async_remote_copy(
            src_ref=buf.at[chunk], dst_ref=buf.at[landing],
            send_sem=send_sem.at[link, slot], recv_sem=recv_sem.at[landing],
            device_id=link_to[link], device_id_type=MESH,
        )

    def leaving(link, slot):
        chunk = look_up(tx[link], slot)
        there = (chunk != NONE) & (chunk // ROW <= y)
        return chunk, (there & (y < 7)) if link == 2 else there

    def send(slot):
        for link in (2, 1, 0):
            chunk, there = leaving(link, slot)
            if link == 1:

                @pl.when((z == 0) & (slot == first_slot(1, 0)))
                def _():
                    pl.semaphore_wait(ready.at[1], 1)

            if link == 0:

                @pl.when(slot == first_up)
                def _():
                    pl.semaphore_wait(ready.at[0], 1)

            @pl.when(there)
            def _(link=link, chunk=chunk):
                move(link, slot, chunk).start()

    pl.semaphore_wait(barrier, 8 + jnp.where(z > 0, 1, 0) + jnp.where(z == 7, 1, 0))

    @pl.when(z > 0)
    def _():
        signal(ready.at[0], device(dz=-1))

    @pl.when(z == 7)
    def _():
        signal(ready.at[1], device(dz=1))

    for t in trades[:4]:
        t.start()
    for copy in local[:4]:
        copy.wait()
    send(jnp.int32(0))
    trades[4].start()

    local[5].wait()
    lane = lax.broadcasted_iota(jnp.int32, (1, HEAD_DIM), 1)
    starts = jnp.zeros((1, HEAD_DIM), jnp.int32)
    ends = jnp.zeros((1, HEAD_DIM), jnp.int32)
    end = jnp.int32(0)
    for i in range(DOCS):
        starts = jnp.where(lane == i, end, starts)
        end = end + lengths[i]
        ends = jnp.where(lane == i, end, ends)
    bounds[0:1, :] = starts
    bounds[1:2, :] = ends

    def in_document(base, rows):
        pos = base + lax.broadcasted_iota(jnp.int32, (rows, HEAD_DIM), 0)
        return (pos >= bounds[0:1, :]) & (pos < bounds[1:2, :])

    q_base = [(ctx - core + lax.rem(core + half, 2)) * ROWS for half in range(2)]
    for half in range(2):
        one_hot = jnp.where(in_document(q_base[half], ROWS), 1.0, 0.0).astype(jnp.bfloat16)
        for g in range(GROUP):
            b = 2 * g + half
            q_all[b * ROWS : (b + 1) * ROWS, HEAD_DIM:] = one_hot
    local[4].wait()
    for t in trades[:4]:
        t.wait_recv()
    send(jnp.int32(1))
    trades[4].wait_recv()
    for half, q_half in enumerate((q_near, q_far)):
        for g in range(GROUP):
            b = 2 * g + half
            q_all[b * ROWS : (b + 1) * ROWS, :HEAD_DIM] = q_half[
                :, g * HEAD_DIM : (g + 1) * HEAD_DIM
            ]

    halves = (slice(0, HEAD_DIM), slice(HEAD_DIM, 2 * HEAD_DIM))

    def load(chunks):
        keys, values = [], []
        for chunk, base in chunks:
            apart = jnp.where(in_document(base, CHUNK), 0.0, -APART).astype(jnp.bfloat16)
            keys.append(jnp.concatenate([buf[chunk, :CHUNK, :], apart], axis=1))
            ones = jnp.ones((CHUNK, HEAD_DIM), jnp.bfloat16)
            values.append(jnp.concatenate([buf[chunk, CHUNK:, :], ones], axis=1))
        keys = [jnp.concatenate(keys[i : i + 2], axis=0) for i in range(0, len(keys), 2)]
        return keys, jnp.concatenate(values, axis=0)

    def attend(b, keys, values, bases=None):
        rows = slice(b * ROWS, (b + 1) * ROWS)
        q = q_all[rows, :]
        scores = []
        for k in keys:
            s = lax.dot_general(
                q, k, (((1,), (1,)), ((), ())), preferred_element_type=jnp.float32
            )
            scores += [s[:, i : i + CHUNK] for i in range(0, k.shape[0], CHUNK)]
        if bases is not None:
            q_pos = q_base[b % 2] + lax.broadcasted_iota(jnp.int32, (ROWS, CHUNK), 0)
            lane_pos = lax.broadcasted_iota(jnp.int32, (ROWS, CHUNK), 1)
            scores = [
                jnp.where(base + lane_pos <= q_pos, s, NEG) for s, base in zip(scores, bases)
            ]
        top = scores[0]
        for s in scores[1:]:
            top = jnp.maximum(top, s)
        top = jnp.max(top, axis=1, keepdims=True)
        if bases is None:
            before = peak[rows, :]
            top = jnp.maximum(before, top)
            factor = jnp.exp2((before - top) * TO_EXP2)
        else:
            top = jnp.broadcast_to(top, (ROWS, HEAD_DIM))
        weights = [jnp.exp2((s - top) * TO_EXP2).astype(jnp.bfloat16) for s in scores]
        update = jnp.dot(
            jnp.concatenate(weights, axis=1), values, preferred_element_type=jnp.float32
        )
        peak[rows, :] = top
        for h in halves:
            acc[rows, h] = update[:, h] if bases is not None else acc[rows, h] * factor + update[:, h]

    def base_of(chunk, there):
        back, s, part = chunk // ROW, lax.rem(chunk // PARTS, 8), lax.rem(chunk, PARTS)
        base = (((y - back) * 8 + s) * 2 + lax.rem(part // 2 + core, 2)) * ROWS
        return jnp.where(there, base + lax.rem(part, 2) * CHUNK, -ROWS)

    bases = [q_base[i // 2] + (i % 2) * CHUNK for i in range(PARTS)]
    keys, values = load([(own + i, base) for i, base in enumerate(bases)])
    for b in range(2 * GROUP):
        attend(b, keys, values, bases)
        if b % GROUP == 0:
            for slot in range(2 + b // GROUP, LEAD, 2):
                send(jnp.int32(slot))

    def arrived(slot):
        chunks, some = [], False
        for link in range(3):
            chunk = look_up(rx[link], slot)
            there = (chunk != NONE) & (chunk // ROW <= y)
            safe = jnp.where(there, chunk, own)

            @pl.when(there)
            def _(safe=safe):
                pltpu.make_async_remote_copy(
                    src_ref=buf.at[safe], dst_ref=buf.at[safe],
                    send_sem=send_sem.at[0, slot], recv_sem=recv_sem.at[safe],
                    device_id=other, device_id_type=MESH,
                ).wait_recv()

            chunks.append((safe, base_of(chunk, there)))
            some = there | some
        return chunks, some

    def step(pair, carry):
        chunks, some = arrived(2 * pair)
        send(2 * pair + LEAD)
        more, any_more = arrived(2 * pair + 1)
        some = some | any_more
        send(2 * pair + LEAD + 1)

        @pl.when(some)
        def _():
            keys, values = load(chunks + more)
            for b in range(2 * GROUP):
                attend(b, keys, values)

        return carry

    lax.fori_loop(0, PAIRS, step, 0)

    last = []
    for slot in range(2 * PAIRS, SLOTS):
        last += arrived(jnp.int32(slot))[0]
        send(jnp.int32(slot + LEAD))

    def send_rest(slot, carry):
        send(slot)
        return carry

    lax.fori_loop(SLOTS + LEAD, SENDS, send_rest, 0)

    share = ROWS // 4
    sends = []
    keys, values = load(last)
    for b in range(2 * GROUP):
        attend(b, keys, values)
        g, half = b // 2, b % 2
        rows = slice(b * ROWS, (b + 1) * ROWS)
        staged[rows, :] = (acc[rows, :HEAD_DIM] / acc[rows, HEAD_DIM:]).astype(jnp.bfloat16)
        spot = pl.ds(pl.multiple_of((2 * x + core) * width + g * HEAD_DIM, HEAD_DIM), HEAD_DIM)
        for dx in range(4):
            to = lax.rem(x + dx, 4)
            piece = pl.ds(pl.multiple_of(b * ROWS + to * share, share), share)
            if half + dx == 0:
                out_ref[:, spot] = staged[piece, :]
                continue
            copy = pltpu.make_async_remote_copy(
                src_ref=staged.at[piece], dst_ref=out_ref.at[:, spot],
                send_sem=out_send.at[b, dx], recv_sem=out_recv.at[b, dx],
                device_id=device(dcore=half, dx=dx), device_id_type=MESH,
            )
            copy.start()
            sends.append(copy)

    for b in (1, 3, 5, 0, 2, 4):
        rows = slice(b * ROWS, (b + 1) * ROWS)
        log = (peak[rows, :] * SCALE + jnp.log(acc[rows, HEAD_DIM:])).T
        log_out[b % 2, b // 2 : b // 2 + 1, :] = log[:1, :]
        if b == 5:
            log_copy = pltpu.make_async_remote_copy(
                src_ref=log_out.at[1], dst_ref=log_in,
                send_sem=log_sem.at[0], recv_sem=log_sem.at[1],
                device_id=other, device_id_type=MESH,
            )
            log_copy.start()

    for t in trades:
        t.wait_send()

    def drain(slot, carry):
        for link in range(3):
            chunk, there = leaving(link, slot)

            @pl.when(there)
            def _(link=link, chunk=chunk):
                move(link, slot, chunk).wait_send()

        return carry

    lax.fori_loop(0, SENDS, drain, 0)
    log_copy.wait()
    near, far = log_out[0, :GROUP, :], log_in[:GROUP, :]
    log_ref[:GROUP, :] = jnp.where(core == 0, near, far)
    log_ref[GROUP:, :] = jnp.where(core == 0, far, near)
    for copy in sends:
        copy.wait()


def on_device(queries, keys, values, doc_lengths):
    columns = 4 * queries.shape[1]
    dma = pltpu.SemaphoreType.DMA
    bf16, f32 = jnp.bfloat16, jnp.float32
    vmem = pl.BlockSpec(memory_space=pltpu.VMEM)
    return pl.pallas_call(
        kernel,
        out_shape=(
            jax.ShapeDtypeStruct((ROWS // 4, columns), bf16),
            jax.ShapeDtypeStruct((2 * GROUP, ROWS), f32),
        ),
        in_specs=[pl.BlockSpec(memory_space=pltpu.HBM)] * 4,
        out_specs=(vmem, vmem),
        scratch_shapes=[
            pltpu.VMEM((3 * ROW, 2 * CHUNK, HEAD_DIM), bf16),
            pltpu.VMEM((ROWS, GROUP * HEAD_DIM), bf16),
            pltpu.VMEM((ROWS, GROUP * HEAD_DIM), bf16),
            pltpu.VMEM((2 * GROUP * ROWS, 2 * HEAD_DIM), bf16),
            pltpu.VMEM((2 * GROUP * ROWS, 2 * HEAD_DIM), f32),
            pltpu.VMEM((2 * GROUP * ROWS, HEAD_DIM), f32),
            pltpu.VMEM((8, HEAD_DIM), jnp.int32),
            pltpu.SMEM((DOCS,), jnp.int32),
            pltpu.VMEM((2 * GROUP * ROWS, HEAD_DIM), bf16),
            pltpu.VMEM((2, 8, ROWS), f32),
            pltpu.VMEM((8, ROWS), f32),
            dma((3, SENDS)),
            dma((3 * ROW,)),
            pltpu.SemaphoreType.REGULAR((2,)),
            dma((6,)),
            dma((5,)),
            dma((5,)),
            dma((2 * GROUP, 4)),
            dma((2 * GROUP, 4)),
            dma((2,)),
        ],
        compiler_params=pltpu.CompilerParams(
            collective_id=0, has_side_effects=True, vmem_limit_bytes=int(63.9 * 2**20)
        ),
        cost_estimate=pl.CostEstimate(
            flops=8 * 10**9, bytes_accessed=2 * 10**6, transcendentals=14 * 10**6
        ),
    )(queries, keys, values, doc_lengths)


def solution(mesh):
    in_specs = (P("ctx", "tp"), P("ctx", "tp"), P("ctx", "tp"), P())
    out_specs = (P(("ctx", "tp"), None), P("tp", "ctx"))
    return jax.shard_map(
        on_device, mesh=mesh, in_specs=in_specs, out_specs=out_specs, check_vma=False
    )
```
